32 devices in a mesh: section: 4 (over y, core), dp: 8 (over z, x).
Axes of the slice: x: 2, y: 2, z: 4, core: 2. Of those that a mesh axis runs over, the one named last changes fastest.
Arguments:
- activations: bfloat16 [4, 2048, 8192], P('section', 'dp'), may hold values from -600 to 600, as said below
- tail_grads: bfloat16 [4, 2048, 512], P('section', 'dp'), may hold values from -48 to 48, as said below
- tail_slots: int32 [4, 8, 4], P('section', 'dp'), may hold values from 0 to 3, each once within a row
- master: float32 [4, 8192, 512], P('section', 'dp'), may hold values from -6 to 6
- moment1: float32 [4, 8192, 512], P('section', 'dp'), may hold values from -0.00029296876 to 0.00029296876
- moment2: float32 [4, 8192, 512], P('section', 'dp'), may hold values from 1.1920929e-09 to 2.9802322e-08
- overflow: int32 [4, 8], P('section', 'dp'), may hold values from 0 to 1, as said below
- clip_on: int32 [4], P('section'), may hold values from 0 to 1, as said below
- next_inputs: bfloat16 [4, 256, 8192], P('section', 'dp'), may hold values from -6 to 6
Outputs:
- new_master: float32 [4, 8192, 512], P('section', 'dp')
- next_out: bfloat16 [4, 256, 512], P('section', 'dp')
The draws below stay inside these ranges and needn't reach their ends.
Inputs may be any that keep to these rules, and one draw needn't show every extreme that they name: `tail_slots`: each row along the last dimension names every slot once. `overflow`: at least one shard is flagged and at least one is not. `clip_on`: at least one section is clipped and at least one is not. `activations`: real-valued. `tail_grads`: real-valued.
All inputs are finite; a program needn't handle non-finite values.
Results may differ from the reference program's by a relative error of at most 0.0049.
Values may be sent and summed in bfloat16 or wider, within the bound.
A program may use at most 64 MiB of HBM per device.

```python
import math
import jax
import jax.numpy as jnp
from jax import lax

D = 8192
TAILS = 4
TAIL_TOK = 64
COLS = 512
TOK_DEV = 256
TOKENS = 2048
NEXT_ALL = 256
N_SECTION = 4
N_DP = 8


def draw_activations(key, part):
    keys = jax.random.split(jax.random.fold_in(key, 11), 3)
    shape = (N_SECTION, TOKENS, D)
    position = jnp.arange(D, dtype=jnp.float32) / D
    rough = jax.random.uniform(keys[1], (N_SECTION, 1, D), jnp.float32, 0.6, 1.4)
    base = jax.random.truncated_normal(keys[0], -4.0, 4.0, shape, jnp.float32)
    column = 10.0 ** position * rough
    section_scale = 1.0 + 2.0 * jnp.arange(N_SECTION, dtype=jnp.float32) / max(N_SECTION - 1, 1)

    def pairing_of(sub):
        return jax.random.permutation(sub, N_DP)
    pairing = jax.vmap(pairing_of)(jax.random.split(keys[2], N_SECTION))
    row_owner = jnp.arange(TOKENS, dtype=jnp.int32) // TOK_DEV
    col_block = jnp.arange(D, dtype=jnp.int32) // (D // N_DP)
    matched = pairing[:, row_owner]
    spike = jnp.where(matched[:, :, None] == col_block[None, None, :], 3.0, 1.0)
    return (base * column * section_scale[:, None, None] * spike).astype(jnp.bfloat16)


def draw_tail_grads(key, part):
    keys = jax.random.split(jax.random.fold_in(key, 23), 2)
    shape = (N_SECTION, TOKENS, COLS)
    spread = jax.random.uniform(keys[1], (N_SECTION, 1, COLS), jnp.float32, 0.0, 1.0)
    base = jax.random.truncated_normal(keys[0], -4.0, 4.0, shape, jnp.float32)
    column = 10.0 ** spread
    return (base * column).astype(jnp.bfloat16)


def section_marks(key, salt, lowest, highest):
    keys = jax.random.split(jax.random.fold_in(key, salt), 2)
    count = jax.random.randint(keys[0], (), lowest, highest + 1, dtype=jnp.int32)
    order = jax.random.permutation(keys[1], N_SECTION).astype(jnp.int32)
    return (order < count).astype(jnp.int32)


def draw_overflow(key, part):
    keys = jax.random.split(jax.random.fold_in(key, 53), 2)
    total = N_SECTION * N_DP
    marks = (jax.random.randint(keys[0], (total,), 0, 4, dtype=jnp.int32) == 0).astype(jnp.int32)
    order = jax.random.permutation(keys[1], total).astype(jnp.int32)
    marks = marks.at[order[0]].set(1)
    marks = marks.at[order[1]].set(0)
    return marks.reshape(N_SECTION, N_DP)


def draw_clip_on(key, part):
    return section_marks(key, 41, 1, max(N_SECTION - 1, 1))


def shard_levels(stream_key, extent, pieces, least, high):
    def one(dim, parts):
        draws = jax.random.uniform(jax.random.fold_in(jax.random.fold_in(stream_key, 6), dim), (parts,), jnp.float32, least / len(pieces), high / len(pieces))
        return jnp.repeat(jnp.exp(draws), extent[dim] // parts).reshape((-1,) + (1,) * (len(extent) - dim - 1))

    level = one(*pieces[0])
    for cut in pieces[1:]:
        level = level * one(*cut)
    return level


def noise(key, extent, deviation, limit, cuts=(), kind=jnp.bfloat16):
    entries = jax.random.normal(key, extent, jnp.float32) * deviation
    if len(cuts) > 0:
        entries = shard_levels(key, extent, cuts, -0.22, 0.18) * entries
    return jnp.clip(entries, min=-limit, max=limit).astype(kind)


def setup_inputs(seed: int = 0) -> dict:
    key_of = jax.random.split(jax.random.key(seed), 10)
    activations = draw_activations(jax.random.fold_in(key_of[9], 71), 0)
    tail_grads = draw_tail_grads(jax.random.fold_in(key_of[9], 71), 0)
    tail_slots = jax.vmap(lambda own: jax.random.permutation(own, TAILS))(jax.random.split(key_of[2], N_SECTION * N_DP)).reshape((N_SECTION, N_DP, TAILS)).astype(jnp.int32)
    master = noise(key_of[3], (N_SECTION, D, COLS), 1.0, 6.0, ((0, 4), (1, 8)), jnp.float32)
    moment1 = noise(key_of[4], (N_SECTION, D, COLS), (0.2 / (N_SECTION * D * COLS) ** 0.5), 0.00029296876, ((0, 4), (1, 8)), jnp.float32)
    moment2 = jnp.clip(jnp.exp(math.log(2.9802322387695312e-08) - 3.218876 * jax.random.uniform(key_of[5], (N_SECTION, D, COLS), jnp.float32) ** shard_levels(key_of[5], (N_SECTION, D, COLS), ((0, 4), (1, 8)), -0.2, 0.2)), 1.19209286886246e-09, 2.9802322387695312e-08)
    overflow = draw_overflow(jax.random.fold_in(key_of[9], 71), 0)
    clip_on = draw_clip_on(jax.random.fold_in(key_of[9], 71), 0)
    next_inputs = noise(key_of[8], (N_SECTION, NEXT_ALL, D), 1.0, 6.0, ((0, 4), (1, 8)))
    return dict(activations=activations, tail_grads=tail_grads, tail_slots=tail_slots, master=master, moment1=moment1, moment2=moment2, overflow=overflow, clip_on=clip_on, next_inputs=next_inputs)


beta_one = 0.9
beta_two = 0.95
correct_one = 1.0 - 0.9 ** 20
correct_two = 1.0 - 0.95 ** 20
adam_eps = 1e-08
decay_rate = 0.1
learn_rate = 0.1

def section_gradient(operands):
    stashed, tails, slots = operands
    onehot = (slots[:, :, None] == jnp.arange(TAILS, dtype=jnp.int32)[None, None, :]).astype(jnp.float32)
    shaped = tails.reshape(N_DP, TAILS, TAIL_TOK, COLS).astype(jnp.float32)
    paired = jnp.einsum('etk,etnc->eknc', onehot, shaped).astype(jnp.bfloat16).reshape(TOKENS, COLS)
    summed = lax.dot_general(stashed, paired, (((0,), (0,)), ((), ())), preferred_element_type=jnp.float32)
    return summed * (1.0 / TOKENS)

def section_forward(operands):
    inputs, weights = operands
    return jnp.dot(inputs, weights, preferred_element_type=jnp.float32)

def reference(activations, tail_grads, tail_slots, master, moment1, moment2, overflow, clip_on, next_inputs):
    grads = lax.map(section_gradient, (activations, tail_grads, tail_slots))
    keep_shard = (overflow == 0).astype(jnp.float32)
    keep = jnp.repeat(keep_shard, D // N_DP, axis=1)
    sumsq = jnp.sum(keep[:, :, None] * (grads * grads))
    norm_value = jnp.sqrt(sumsq)
    factor = jnp.where(clip_on == 1, 1.0 / jnp.maximum(norm_value, 1.0), 1.0).astype(jnp.float32)
    clipped = grads * factor[:, None, None]
    m_next = beta_one * moment1 + (1.0 - beta_one) * clipped
    v_next = beta_two * moment2 + (1.0 - beta_two) * (clipped * clipped)
    update = m_next / correct_one / (jnp.sqrt(v_next / correct_two) + adam_eps) + decay_rate * master
    new_master = jnp.where(keep[:, :, None] > 0.5, master - learn_rate * update, master)
    weights = new_master.astype(jnp.bfloat16)
    result = lax.map(section_forward, (next_inputs, weights))
    next_out = (result * (1.0 / math.sqrt(D))).astype(jnp.bfloat16)
    return (new_master, next_out)
```

```python
import functools
import math

import jax
import jax.numpy as jnp
from jax import lax
from jax.experimental import pallas as pl
from jax.experimental.pallas import tpu as pltpu
from jax.sharding import PartitionSpec as P

MESH = pl.DeviceIdType.MESH
beta_one = 0.9
beta_two = 0.95
correct_one = 1.0 - 0.9**20
correct_two = 1.0 - 0.95**20
adam_eps = 1e-08
decay_rate = 0.1
learn_rate = 0.1


def remote(src, dst, send, recv, where):
    return pltpu.make_async_remote_copy(
        src_ref=src, dst_ref=dst, send_sem=send, recv_sem=recv, device_id=where,
        device_id_type=MESH,
    )


def kernel(
    n, sections, step,
    act, tails, slots, master_in, m1_in, m2_in, overflow, clip_on, nxt,
    master_out, next_out,
    far, near, paired, master, m1, m2, grad, psend, precv, weights, inputs, part, landed,
    sq_dp, sq_sec, sq_mine, sq_sum,
    load_sem, far_s, far_r, near_s, near_r, pair_s, pair_r, p_s, p_r, in_s, in_r, out_s, out_r,
    sd_s, sd_r, ss_s, ss_r,
):
    tok, width = act.shape
    rows, cols = master.shape
    nrows = nxt.shape[0]
    tail_count = slots.shape[-1]
    tail_tok = tok // tail_count
    group = n // 2
    me = lax.axis_index("dp")
    sec = lax.axis_index("section")
    half = me // group
    low = lax.rem(me, group)
    other = 1 - half
    pieces = rows // step

    def each(count, body):
        lax.fori_loop(1, count, lambda j, c: (body(j), c)[1], 0)

    barrier = pltpu.get_barrier_semaphore()
    each(n, lambda j: pl.semaphore_signal(
        barrier, inc=1, device_id={"dp": lax.rem(me + j, n)}, device_id_type=MESH))
    each(sections, lambda j: pl.semaphore_signal(
        barrier, inc=1, device_id={"section": lax.rem(sec + j, sections)}, device_id_type=MESH))

    def feature(dev):
        return pl.ds(pl.multiple_of(dev * rows, rows), rows)

    def block(ref, index, size):
        return ref.at[pl.ds(pl.multiple_of(index * size, size), size)]

    loads = [
        pltpu.make_async_copy(
            act.at[:, feature(other * group + low)], block(far, low, tok), load_sem.at[0]),
        pltpu.make_async_copy(
            act.at[:, feature(me)], block(near, low, tok), load_sem.at[1]),
        pltpu.make_async_copy(
            nxt.at[:, feature(me)], block(inputs, me, nrows), load_sem.at[2]),
        pltpu.make_async_copy(master_in, master, load_sem.at[3]),
        pltpu.make_async_copy(m1_in, m1, load_sem.at[4]),
        pltpu.make_async_copy(m2_in, m2, load_sem.at[5]),
    ]
    for load in loads:
        load.start()

    mine = pl.multiple_of(low * tok, tok)
    for k in range(tail_count):
        value = tails[0:tail_tok, :]
        for t in range(1, tail_count):
            value = jnp.where(
                slots[0, t] == k, tails[t * tail_tok:(t + 1) * tail_tok, :], value)
        paired[pl.ds(mine + k * tail_tok, tail_tok), :] = value

    pl.semaphore_wait(barrier, n - 1 + sections - 1)

    def peer(j):
        return lax.rem(low + j, group)

    def pair_copy(to, slot):
        return remote(block(paired, low, tok), block(paired, slot, tok), pair_s.at[to],
                      pair_r.at[slot], {"dp": half * group + to})

    def far_copy(to, slot):
        return remote(act.at[:, feature(other * group + to)], block(far, slot, tok),
                      far_s.at[to], far_r.at[slot], {"dp": half * group + to})

    def near_copy(to, slot):
        return remote(act.at[:, feature(half * group + to)], block(near, slot, tok),
                      near_s.at[to], near_r.at[slot], {"dp": half * group + to})

    each(group, lambda j: pair_copy(peer(j), low).start())
    each(group, lambda j: far_copy(peer(j), low).start())
    each(group, lambda j: near_copy(peer(j), low).start())

    contract = (((0,), (0,)), ((), ()))

    loads[0].wait()
    each(group, lambda j: pair_copy(peer(j), peer(j)).wait_recv())
    each(group, lambda j: far_copy(peer(j), peer(j)).wait_recv())

    def part_copy(c):
        return remote(psend.at[c], precv.at[c], p_s.at[c], p_r.at[c],
                      {"dp": other * group + low})

    for c in range(pieces):
        psend[c] = lax.dot_general(
            far[:, c * step:(c + 1) * step], paired[...], contract,
            preferred_element_type=jnp.float32).astype(psend.dtype)
        part_copy(c).start()

    def input_copy(to, slot):
        return remote(nxt.at[:, feature(to)], block(inputs, slot, nrows), in_s.at[to],
                      in_r.at[slot], {"dp": to})

    def other_dp(j):
        return lax.rem(me + j, n)

    each(n, lambda j: input_copy(other_dp(j), me).start())

    loads[1].wait()
    each(group, lambda j: near_copy(peer(j), peer(j)).wait_recv())
    for c in range(pieces):
        grad[c * step:(c + 1) * step, :] = lax.dot_general(
            near[:, c * step:(c + 1) * step], paired[...], contract,
            preferred_element_type=jnp.float32)

    scale = 1.0 / (tok * n)
    chunk = 32
    squares = jnp.zeros((8, cols), jnp.float32)
    for c in range(pieces):
        part_copy(c).wait_recv()

        def add(i, total):
            at = pl.multiple_of(i * chunk, chunk)
            g = (grad[pl.ds(c * step + at, chunk), :]
                 + precv[c, pl.ds(at, chunk), :].astype(jnp.float32)) * scale
            grad[pl.ds(c * step + at, chunk), :] = g
            return total + jnp.sum((g * g).reshape(chunk // 8, 8, cols), axis=0)

        squares = lax.fori_loop(0, step // chunk, add, squares)

    tile = squares[:, 0:128]
    for c in range(1, cols // 128):
        tile = tile + squares[:, c * 128:(c + 1) * 128]
    keep = jnp.where(overflow[0, 0] == 0, 1.0, 0.0)
    tile = tile * keep
    sq_mine[...] = tile

    def sq_copy(to, slot):
        return remote(sq_mine, sq_dp.at[slot], sd_s.at[to], sd_r.at[slot], {"dp": to})

    def sum_copy(to, slot):
        return remote(sq_sum, sq_sec.at[slot], ss_s.at[to], ss_r.at[slot], {"section": to})

    def other_section(j):
        return lax.rem(sec + j, sections)

    each(n, lambda j: sq_copy(other_dp(j), me).start())
    sq_dp[me] = tile
    for load in loads[2:]:
        load.wait()
    each(n, lambda j: sq_copy(other_dp(j), other_dp(j)).wait_recv())
    tile = jnp.sum(sq_dp[...], axis=0)
    sq_sum[...] = tile
    each(sections, lambda j: sum_copy(other_section(j), sec).start())
    sq_sec[sec] = tile
    each(sections, lambda j: sum_copy(other_section(j), other_section(j)).wait_recv())
    sumsq = jnp.sum(jnp.sum(sq_sec[...], axis=0), keepdims=True)
    factor = jnp.where(clip_on[0] == 1, 1.0 / jnp.maximum(jnp.sqrt(sumsq), 1.0), 1.0)
    factor = jnp.broadcast_to(factor, (1, cols))
    rate = learn_rate * keep

    def update(i, carry):
        at = pl.ds(pl.multiple_of(i * chunk, chunk), chunk)
        clipped = grad[at, :] * factor
        old = master[at, :]
        m_next = beta_one * m1[at, :] + (1.0 - beta_one) * clipped
        v_next = beta_two * m2[at, :] + (1.0 - beta_two) * (clipped * clipped)
        change = (m_next * (1.0 / correct_one)) / (
            jnp.sqrt(v_next * (1.0 / correct_two)) + adam_eps) + decay_rate * old
        new = old - rate * change
        master[at, :] = new
        weights[at, :] = new.astype(weights.dtype)
        return carry

    lax.fori_loop(0, rows // chunk, update, 0)
    store = pltpu.make_async_copy(master, master_out, load_sem.at[6])
    store.start()

    each(n, lambda j: input_copy(other_dp(j), other_dp(j)).wait_recv())
    part[...] = jnp.dot(inputs[...], weights[...], preferred_element_type=jnp.float32)

    def out_copy(to, slot):
        return remote(block(part, to, nrows), landed.at[slot], out_s.at[to], out_r.at[slot],
                      {"dp": to})

    each(n, lambda j: out_copy(other_dp(j), me).start())
    landed[me] = part[pl.ds(pl.multiple_of(me * nrows, nrows), nrows), :]
    each(n, lambda j: out_copy(other_dp(j), other_dp(j)).wait_recv())
    next_out[...] = (
        jnp.sum(landed[...], axis=0) * (1.0 / math.sqrt(width))).astype(next_out.dtype)

    each(group, lambda j: pair_copy(peer(j), low).wait_send())
    each(group, lambda j: far_copy(peer(j), low).wait_send())
    each(group, lambda j: near_copy(peer(j), low).wait_send())
    for c in range(pieces):
        part_copy(c).wait_send()
    each(n, lambda j: input_copy(other_dp(j), me).wait_send())
    each(n, lambda j: sq_copy(other_dp(j), me).wait_send())
    each(sections, lambda j: sum_copy(other_section(j), sec).wait_send())
    each(n, lambda j: out_copy(other_dp(j), me).wait_send())
    store.wait()


def local(
    activations, tail_grads, tail_slots, master, moment1, moment2, overflow, clip_on, next_inputs
):
    n = lax.axis_size("dp")
    sections = lax.axis_size("section")
    tok = activations.shape[1]
    rows, cols = master.shape[1:]
    nrows = next_inputs.shape[1]
    group = n // 2
    step = min(rows, 256)
    pieces = rows // step
    f32, bf16 = jnp.float32, jnp.bfloat16
    vmem, anywhere, smem = (
        pl.BlockSpec(memory_space=m) for m in (pltpu.VMEM, pl.ANY, pltpu.SMEM))
    dma = pltpu.SemaphoreType.DMA
    new_master, next_out = pl.pallas_call(
        functools.partial(kernel, n, sections, step),
        out_shape=(
            jax.ShapeDtypeStruct((rows, cols), f32),
            jax.ShapeDtypeStruct((nrows, cols), bf16),
        ),
        in_specs=[anywhere, vmem, smem, anywhere, anywhere, anywhere, smem, smem, anywhere],
        out_specs=(anywhere, vmem),
        scratch_shapes=[
            pltpu.VMEM((group * tok, rows), bf16),
            pltpu.VMEM((group * tok, rows), bf16),
            pltpu.VMEM((group * tok, cols), bf16),
            pltpu.VMEM((rows, cols), f32),
            pltpu.VMEM((rows, cols), f32),
            pltpu.VMEM((rows, cols), f32),
            pltpu.VMEM((rows, cols), f32),
            pltpu.VMEM((pieces, step, cols), bf16),
            pltpu.VMEM((pieces, step, cols), bf16),
            pltpu.VMEM((rows, cols), bf16),
            pltpu.VMEM((n * nrows, rows), bf16),
            pltpu.VMEM((n * nrows, cols), f32),
            pltpu.VMEM((n, nrows, cols), f32),
            pltpu.VMEM((n, 8, 128), f32),
            pltpu.VMEM((sections, 8, 128), f32),
            pltpu.VMEM((8, 128), f32),
            pltpu.VMEM((8, 128), f32),
            dma((7,)),
            dma((group,)), dma((group,)),
            dma((group,)), dma((group,)),
            dma((group,)), dma((group,)),
            dma((pieces,)), dma((pieces,)),
            dma((n,)), dma((n,)),
            dma((n,)), dma((n,)),
            dma((n,)), dma((n,)),
            dma((sections,)), dma((sections,)),
        ],
        compiler_params=pltpu.CompilerParams(
            collective_id=0, has_side_effects=True, vmem_limit_bytes=56 * 1024 * 1024),
    )(
        activations[0], tail_grads[0], tail_slots[0], master[0], moment1[0], moment2[0],
        overflow, clip_on, next_inputs[0],
    )
    return (new_master[None], next_out[None])


def solution(mesh):
    return jax.shard_map(
        local,
        mesh=mesh,
        in_specs=(
            P("section", "dp", None),
            P("section", "dp", None),
            P("section", "dp", None),
            P("section", "dp", None),
            P("section", "dp", None),
            P("section", "dp", None),
            P("section", "dp"),
            P("section"),
            P("section", "dp", None),
        ),
        out_specs=(P("section", "dp", None), P("section", "dp", None)),
        check_vma=False,
    )
```

```python
import functools
import math

import jax
import jax.numpy as jnp
from jax import lax
from jax.experimental import pallas as pl
from jax.experimental.pallas import tpu as pltpu
from jax.sharding import PartitionSpec as P

MESH = pl.DeviceIdType.MESH
beta_one = 0.9
beta_two = 0.95
correct_one = 1.0 - 0.9**20
correct_two = 1.0 - 0.95**20
adam_eps = 1e-08
decay_rate = 0.1
learn_rate = 0.1


def remote(src, dst, send, recv, where):
    return pltpu.make_async_remote_copy(
        src_ref=src, dst_ref=dst, send_sem=send, recv_sem=recv, device_id=where,
        device_id_type=MESH,
    )


def kernel(
    n, sections, step,
    act, tails, slots, master_in, m1_in, m2_in, overflow, clip_on, nxt,
    master_out, next_out,
    far, near, paired, master, m1, m2, grad, psend, precv, weights, inputs, part, landed,
    sq_dp, sq_sec, sq_mine, sq_sum,
    load_sem, far_s, far_r, near_s, near_r, pair_s, pair_r, p_s, p_r, in_s, in_r, out_s, out_r,
    sd_s, sd_r, ss_s, ss_r, relay_s,
):
    tok, width = act.shape
    rows, cols = master.shape
    nrows = nxt.shape[0]
    tail_count = slots.shape[-1]
    tail_tok = tok // tail_count
    group = n // 2
    me = lax.axis_index("dp")
    sec = lax.axis_index("section")
    half = me // group
    low = lax.rem(me, group)
    other = 1 - half
    pieces = rows // step

    def each(count, body):
        lax.fori_loop(1, count, lambda j, c: (body(j), c)[1], 0)

    barrier = pltpu.get_barrier_semaphore()
    each(n, lambda j: pl.semaphore_signal(
        barrier, inc=1, device_id={"dp": lax.rem(me + j, n)}, device_id_type=MESH))
    each(sections, lambda j: pl.semaphore_signal(
        barrier, inc=1, device_id={"section": lax.rem(sec + j, sections)}, device_id_type=MESH))

    def feature(dev):
        return pl.ds(pl.multiple_of(dev * rows, rows), rows)

    def block(ref, index, size):
        return ref.at[pl.ds(pl.multiple_of(index * size, size), size)]

    loads = [
        pltpu.make_async_copy(
            act.at[:, feature(other * group + low)], block(far, low, tok), load_sem.at[0]),
        pltpu.make_async_copy(
            act.at[:, feature(me)], block(near, low, tok), load_sem.at[1]),
        pltpu.make_async_copy(
            nxt.at[:, feature(me)], block(inputs, me, nrows), load_sem.at[2]),
        pltpu.make_async_copy(master_in, master, load_sem.at[3]),
        pltpu.make_async_copy(m1_in, m1, load_sem.at[4]),
        pltpu.make_async_copy(m2_in, m2, load_sem.at[5]),
    ]
    for load in loads:
        load.start()

    mine = pl.multiple_of(low * tok, tok)
    for k in range(tail_count):
        value = tails[0:tail_tok, :]
        for t in range(1, tail_count):
            value = jnp.where(
                slots[0, t] == k, tails[t * tail_tok:(t + 1) * tail_tok, :], value)
        paired[pl.ds(mine + k * tail_tok, tail_tok), :] = value

    pl.semaphore_wait(barrier, n - 1 + sections - 1)

    def peer(j):
        return lax.rem(low + j, group)

    def pair_copy(to, slot):
        return remote(block(paired, low, tok), block(paired, slot, tok), pair_s.at[to],
                      pair_r.at[slot], {"dp": half * group + to})

    def far_copy(to, slot):
        return remote(act.at[:, feature(other * group + to)], block(far, slot, tok),
                      far_s.at[to], far_r.at[slot], {"dp": half * group + to})

    def near_copy(to, slot):
        return remote(act.at[:, feature(half * group + to)], block(near, slot, tok),
                      near_s.at[to], near_r.at[slot], {"dp": half * group + to})

    inner = low + 1 - 2 * lax.rem(low, 2)
    outer = group // 2

    def across(j):
        return lax.rem(low + 2 * j, group)

    def relay_copy(slot, held):
        return remote(block(paired, held, tok), block(paired, held, tok), relay_s.at[slot],
                      pair_r.at[held], {"dp": half * group + inner})

    pair_copy(inner, low).start()
    each(outer, lambda j: pair_copy(across(j), low).start())
    each(group, lambda j: far_copy(peer(j), low).start())
    each(group, lambda j: near_copy(peer(j), low).start())

    def relay(j):
        pair_copy(across(j), across(j)).wait_recv()
        relay_copy(j, across(j)).start()

    each(outer, relay)

    contract = (((0,), (0,)), ((), ()))

    loads[0].wait()
    pair_copy(inner, inner).wait_recv()
    each(outer, lambda j: pair_copy(
        inner, lax.rem(inner + 2 * j, group)).wait_recv())
    each(group, lambda j: far_copy(peer(j), peer(j)).wait_recv())

    def part_copy(c):
        return remote(psend.at[c], precv.at[c], p_s.at[c], p_r.at[c],
                      {"dp": other * group + low})

    for c in range(pieces):
        psend[c] = lax.dot_general(
            far[:, c * step:(c + 1) * step], paired[...], contract,
            preferred_element_type=jnp.float32).astype(psend.dtype)
        part_copy(c).start()

    def input_copy(to, slot):
        return remote(nxt.at[:, feature(to)], block(inputs, slot, nrows), in_s.at[to],
                      in_r.at[slot], {"dp": to})

    def other_dp(j):
        return lax.rem(me + j, n)

    loads[1].wait()
    each(group, lambda j: near_copy(peer(j), peer(j)).wait_recv())
    for c in range(pieces):
        grad[c * step:(c + 1) * step, :] = lax.dot_general(
            near[:, c * step:(c + 1) * step], paired[...], contract,
            preferred_element_type=jnp.float32)

    scale = 1.0 / (tok * n)
    chunk = 32
    squares = jnp.zeros((8, cols), jnp.float32)
    for c in range(pieces):
        part_copy(c).wait_recv()

        def add(i, total):
            at = pl.multiple_of(i * chunk, chunk)
            g = (grad[pl.ds(c * step + at, chunk), :]
                 + precv[c, pl.ds(at, chunk), :].astype(jnp.float32)) * scale
            grad[pl.ds(c * step + at, chunk), :] = g
            return total + jnp.sum((g * g).reshape(chunk // 8, 8, cols), axis=0)

        squares = lax.fori_loop(0, step // chunk, add, squares)

    tile = squares[:, 0:128]
    for c in range(1, cols // 128):
        tile = tile + squares[:, c * 128:(c + 1) * 128]
    keep = jnp.where(overflow[0, 0] == 0, 1.0, 0.0)
    tile = tile * keep
    sq_mine[...] = tile

    def sq_copy(to, slot):
        return remote(sq_mine, sq_dp.at[slot], sd_s.at[to], sd_r.at[slot], {"dp": to})

    def sum_copy(to, slot):
        return remote(sq_sum, sq_sec.at[slot], ss_s.at[to], ss_r.at[slot], {"section": to})

    def other_section(j):
        return lax.rem(sec + j, sections)

    each(n, lambda j: sq_copy(other_dp(j), me).start())
    each(n, lambda j: input_copy(other_dp(j), me).start())
    sq_dp[me] = tile
    for load in loads[2:]:
        load.wait()
    each(n, lambda j: sq_copy(other_dp(j), other_dp(j)).wait_recv())
    tile = jnp.sum(sq_dp[...], axis=0)
    sq_sum[...] = tile
    each(sections, lambda j: sum_copy(other_section(j), sec).start())
    sq_sec[sec] = tile
    each(sections, lambda j: sum_copy(other_section(j), other_section(j)).wait_recv())
    sumsq = jnp.sum(jnp.sum(sq_sec[...], axis=0), keepdims=True)
    factor = jnp.where(clip_on[0] == 1, 1.0 / jnp.maximum(jnp.sqrt(sumsq), 1.0), 1.0)
    side = cols // 2
    factor = jnp.broadcast_to(factor, (1, side))
    rate = learn_rate * keep

    def out_copy(h, to, slot):
        return remote(part.at[h, pl.ds(pl.multiple_of(to * nrows, nrows), nrows)],
                      landed.at[h, slot], out_s.at[h, to], out_r.at[h, slot], {"dp": to})

    stores = []
    for h in range(2):
        span = slice(h * side, (h + 1) * side)

        def update(i, carry):
            at = pl.ds(pl.multiple_of(i * chunk, chunk), chunk)
            clipped = grad[at, span] * factor
            old = master[at, span]
            m_next = beta_one * m1[at, span] + (1.0 - beta_one) * clipped
            v_next = beta_two * m2[at, span] + (1.0 - beta_two) * (clipped * clipped)
            change = (m_next * (1.0 / correct_one)) / (
                jnp.sqrt(v_next * (1.0 / correct_two)) + adam_eps) + decay_rate * old
            new = old - rate * change
            master[at, span] = new
            weights[at, span] = new.astype(weights.dtype)
            return carry

        lax.fori_loop(0, rows // chunk, update, 0)
        if h == 0:
            each(n, lambda j: input_copy(other_dp(j), other_dp(j)).wait_recv())
        part[h] = jnp.dot(inputs[...], weights[:, span], preferred_element_type=jnp.float32)
        each(n, lambda j: out_copy(h, other_dp(j), me).start())
        landed[h, me] = part[h, pl.ds(pl.multiple_of(me * nrows, nrows), nrows), :]
        stores.append(pltpu.make_async_copy(
            master.at[:, span], master_out.at[:, span], load_sem.at[6 + h]))
        stores[h].start()

    for h in range(2):
        each(n, lambda j: out_copy(h, other_dp(j), other_dp(j)).wait_recv())
        next_out[:, h * side:(h + 1) * side] = (
            jnp.sum(landed[h], axis=0) * (1.0 / math.sqrt(width))).astype(next_out.dtype)

    pair_copy(inner, low).wait_send()
    each(outer, lambda j: pair_copy(across(j), low).wait_send())
    each(outer, lambda j: relay_copy(j, across(j)).wait_send())
    each(group, lambda j: far_copy(peer(j), low).wait_send())
    each(group, lambda j: near_copy(peer(j), low).wait_send())
    for c in range(pieces):
        part_copy(c).wait_send()
    each(n, lambda j: input_copy(other_dp(j), me).wait_send())
    each(n, lambda j: sq_copy(other_dp(j), me).wait_send())
    each(sections, lambda j: sum_copy(other_section(j), sec).wait_send())
    for h in range(2):
        each(n, lambda j: out_copy(h, other_dp(j), me).wait_send())
        stores[h].wait()


def local(
    activations, tail_grads, tail_slots, master, moment1, moment2, overflow, clip_on, next_inputs
):
    n = lax.axis_size("dp")
    sections = lax.axis_size("section")
    tok = activations.shape[1]
    rows, cols = master.shape[1:]
    nrows = next_inputs.shape[1]
    group = n // 2
    step = min(rows, 256)
    pieces = rows // step
    f32, bf16 = jnp.float32, jnp.bfloat16
    vmem, anywhere, smem = (
        pl.BlockSpec(memory_space=m) for m in (pltpu.VMEM, pl.ANY, pltpu.SMEM))
    dma = pltpu.SemaphoreType.DMA
    new_master, next_out = pl.pallas_call(
        functools.partial(kernel, n, sections, step),
        out_shape=(
            jax.ShapeDtypeStruct((rows, cols), f32),
            jax.ShapeDtypeStruct((nrows, cols), bf16),
        ),
        in_specs=[anywhere, vmem, smem, anywhere, anywhere, anywhere, smem, smem, anywhere],
        out_specs=(anywhere, vmem),
        scratch_shapes=[
            pltpu.VMEM((group * tok, rows), bf16),
            pltpu.VMEM((group * tok, rows), bf16),
            pltpu.VMEM((group * tok, cols), bf16),
            pltpu.VMEM((rows, cols), f32),
            pltpu.VMEM((rows, cols), f32),
            pltpu.VMEM((rows, cols), f32),
            pltpu.VMEM((rows, cols), f32),
            pltpu.VMEM((pieces, step, cols), bf16),
            pltpu.VMEM((pieces, step, cols), bf16),
            pltpu.VMEM((rows, cols), bf16),
            pltpu.VMEM((n * nrows, rows), bf16),
            pltpu.VMEM((2, n * nrows, cols // 2), f32),
            pltpu.VMEM((2, n, nrows, cols // 2), f32),
            pltpu.VMEM((n, 8, 128), f32),
            pltpu.VMEM((sections, 8, 128), f32),
            pltpu.VMEM((8, 128), f32),
            pltpu.VMEM((8, 128), f32),
            dma((8,)),
            dma((group,)), dma((group,)),
            dma((group,)), dma((group,)),
            dma((group,)), dma((group,)),
            dma((pieces,)), dma((pieces,)),
            dma((n,)), dma((n,)),
            dma((2, n)), dma((2, n)),
            dma((n,)), dma((n,)),
            dma((sections,)), dma((sections,)),
            dma((max(group // 2, 1),)),
        ],
        compiler_params=pltpu.CompilerParams(
            collective_id=0, has_side_effects=True, vmem_limit_bytes=56 * 1024 * 1024),
    )(
        activations[0], tail_grads[0], tail_slots[0], master[0], moment1[0], moment2[0],
        overflow, clip_on, next_inputs[0],
    )
    return (new_master[None], next_out[None])


def solution(mesh):
    return jax.shard_map(
        local,
        mesh=mesh,
        in_specs=(
            P("section", "dp", None),
            P("section", "dp", None),
            P("section", "dp", None),
            P("section", "dp", None),
            P("section", "dp", None),
            P("section", "dp", None),
            P("section", "dp"),
            P("section"),
            P("section", "dp", None),
        ),
        out_specs=(P("section", "dp", None), P("section", "dp", None)),
        check_vma=False,
    )
```

```python
import functools
import math

import jax
import jax.numpy as jnp
from jax import lax
from jax.experimental import pallas as pl
from jax.experimental.pallas import tpu as pltpu
from jax.sharding import PartitionSpec as P

MESH = pl.DeviceIdType.MESH
beta_one = 0.9
beta_two = 0.95
correct_one = 1.0 - 0.9**20
correct_two = 1.0 - 0.95**20
adam_eps = 1e-08
decay_rate = 0.1
learn_rate = 0.1


def remote(src, dst, send, recv, where):
    return pltpu.make_async_remote_copy(
        src_ref=src, dst_ref=dst, send_sem=send, recv_sem=recv, device_id=where,
        device_id_type=MESH,
    )


def kernel(
    n, sections, step,
    act, tails, slots, master_in, m1_in, m2_in, overflow, clip_on, nxt,
    master_out, next_out,
    far, near, paired, master, m1, m2, grad, psend, precv, weights, inputs, part, landed,
    sq_dp, sq_sec, sq_mine, sq_sum,
    load_sem, far_s, far_r, near_s, near_r, pair_s, pair_r, p_s, p_r, in_s, in_r, out_s, out_r,
    sd_s, sd_r, ss_s, ss_r,
):
    tok, width = act.shape
    rows, cols = master.shape
    nrows = nxt.shape[0]
    tail_count = slots.shape[-1]
    tail_tok = tok // tail_count
    group = n // 2
    me = lax.axis_index("dp")
    sec = lax.axis_index("section")
    half = me // group
    low = lax.rem(me, group)
    other = 1 - half
    pieces = rows // step

    def each(count, body):
        lax.fori_loop(1, count, lambda j, c: (body(j), c)[1], 0)

    barrier = pltpu.get_barrier_semaphore()
    each(n, lambda j: pl.semaphore_signal(
        barrier, inc=1, device_id={"dp": lax.rem(me + j, n)}, device_id_type=MESH))
    each(sections, lambda j: pl.semaphore_signal(
        barrier, inc=1, device_id={"section": lax.rem(sec + j, sections)}, device_id_type=MESH))

    def feature(dev):
        return pl.ds(pl.multiple_of(dev * rows, rows), rows)

    def block(ref, index, size):
        return ref.at[pl.ds(pl.multiple_of(index * size, size), size)]

    loads = [
        pltpu.make_async_copy(
            act.at[:, feature(other * group + low)], block(far, low, tok), load_sem.at[0]),
        pltpu.make_async_copy(
            act.at[:, feature(me)], block(near, low, tok), load_sem.at[1]),
        pltpu.make_async_copy(
            nxt.at[:, feature(me)], block(inputs, me, nrows), load_sem.at[2]),
        pltpu.make_async_copy(master_in, master, load_sem.at[3]),
        pltpu.make_async_copy(m1_in, m1, load_sem.at[4]),
        pltpu.make_async_copy(m2_in, m2, load_sem.at[5]),
    ]
    for load in loads:
        load.start()

    mine = pl.multiple_of(low * tok, tok)
    for k in range(tail_count):
        value = tails[0:tail_tok, :]
        for t in range(1, tail_count):
            value = jnp.where(
                slots[0, t] == k, tails[t * tail_tok:(t + 1) * tail_tok, :], value)
        paired[pl.ds(mine + k * tail_tok, tail_tok), :] = value

    pl.semaphore_wait(barrier, n - 1 + sections - 1)

    def peer(j):
        return lax.rem(low + j, group)

    def pair_copy(to, slot):
        return remote(block(paired, low, tok), block(paired, slot, tok), pair_s.at[to],
                      pair_r.at[slot], {"dp": half * group + to})

    def far_copy(to, slot):
        return remote(act.at[:, feature(other * group + to)], block(far, slot, tok),
                      far_s.at[to], far_r.at[slot], {"dp": half * group + to})

    def near_copy(to, slot):
        return remote(act.at[:, feature(half * group + to)], block(near, slot, tok),
                      near_s.at[to], near_r.at[slot], {"dp": half * group + to})

    inner = low + 1 - 2 * lax.rem(low, 2)
    outer = group // 2

    def across(j):
        return lax.rem(low + 2 * j, group)

    each(group, lambda j: pair_copy(peer(j), low).start())

    def diagonal(j):
        return lax.rem(inner + 2 * j, group)

    each(outer, lambda j: far_copy(across(j), low).start())
    each(outer, lambda j: far_copy(diagonal(j), low).start())
    far_copy(inner, low).start()
    each(outer, lambda j: near_copy(across(j), low).start())
    each(outer, lambda j: near_copy(diagonal(j), low).start())
    near_copy(inner, low).start()

    contract = (((0,), (0,)), ((), ()))

    loads[0].wait()
    each(group, lambda j: pair_copy(peer(j), peer(j)).wait_recv())
    each(group, lambda j: far_copy(peer(j), peer(j)).wait_recv())

    def part_copy(c):
        return remote(psend.at[c], precv.at[c], p_s.at[c], p_r.at[c],
                      {"dp": other * group + low})

    for c in range(pieces):
        psend[c] = lax.dot_general(
            far[:, c * step:(c + 1) * step], paired[...], contract,
            preferred_element_type=jnp.float32).astype(psend.dtype)
        part_copy(c).start()

    def input_copy(to, slot):
        return remote(nxt.at[:, feature(to)], block(inputs, slot, nrows), in_s.at[to],
                      in_r.at[slot], {"dp": to})

    def other_dp(j):
        return lax.rem(me + j, n)

    loads[1].wait()
    each(group, lambda j: near_copy(peer(j), peer(j)).wait_recv())
    for c in range(pieces):
        grad[c * step:(c + 1) * step, :] = lax.dot_general(
            near[:, c * step:(c + 1) * step], paired[...], contract,
            preferred_element_type=jnp.float32)

    scale = 1.0 / (tok * n)
    chunk = 32
    squares = jnp.zeros((8, cols), jnp.float32)
    for c in range(pieces):
        part_copy(c).wait_recv()

        def add(i, total):
            at = pl.multiple_of(i * chunk, chunk)
            g = (grad[pl.ds(c * step + at, chunk), :]
                 + precv[c, pl.ds(at, chunk), :].astype(jnp.float32)) * scale
            grad[pl.ds(c * step + at, chunk), :] = g
            return total + jnp.sum((g * g).reshape(chunk // 8, 8, cols), axis=0)

        squares = lax.fori_loop(0, step // chunk, add, squares)

    tile = squares[:, 0:128]
    for c in range(1, cols // 128):
        tile = tile + squares[:, c * 128:(c + 1) * 128]
    keep = jnp.where(overflow[0, 0] == 0, 1.0, 0.0)
    tile = tile * keep
    sq_mine[...] = tile

    def sq_copy(to, slot):
        return remote(sq_mine, sq_dp.at[slot], sd_s.at[to], sd_r.at[slot], {"dp": to})

    def sum_copy(to, slot):
        return remote(sq_sum, sq_sec.at[slot], ss_s.at[to], ss_r.at[slot], {"section": to})

    def other_section(j):
        return lax.rem(sec + j, sections)

    each(n, lambda j: sq_copy(other_dp(j), me).start())
    each(n, lambda j: input_copy(other_dp(j), me).start())
    sq_dp[me] = tile
    for load in loads[2:]:
        load.wait()
    each(n, lambda j: sq_copy(other_dp(j), other_dp(j)).wait_recv())
    tile = jnp.sum(sq_dp[...], axis=0)
    sq_sum[...] = tile
    each(sections, lambda j: sum_copy(other_section(j), sec).start())
    sq_sec[sec] = tile
    each(sections, lambda j: sum_copy(other_section(j), other_section(j)).wait_recv())
    sumsq = jnp.sum(jnp.sum(sq_sec[...], axis=0), keepdims=True)
    factor = jnp.where(clip_on[0] == 1, 1.0 / jnp.maximum(jnp.sqrt(sumsq), 1.0), 1.0)
    side = cols // 2
    factor = jnp.broadcast_to(factor, (1, side))
    rate = learn_rate * keep

    def out_copy(h, to, slot):
        return remote(part.at[h, pl.ds(pl.multiple_of(to * nrows, nrows), nrows)],
                      landed.at[h, slot], out_s.at[h, to], out_r.at[h, slot], {"dp": to})

    stores = []
    for h in range(2):
        span = slice(h * side, (h + 1) * side)

        def update(i, carry):
            at = pl.ds(pl.multiple_of(i * chunk, chunk), chunk)
            clipped = grad[at, span] * factor
            old = master[at, span]
            m_next = beta_one * m1[at, span] + (1.0 - beta_one) * clipped
            v_next = beta_two * m2[at, span] + (1.0 - beta_two) * (clipped * clipped)
            change = (m_next * (1.0 / correct_one)) / (
                jnp.sqrt(v_next * (1.0 / correct_two)) + adam_eps) + decay_rate * old
            new = old - rate * change
            master[at, span] = new
            weights[at, span] = new.astype(weights.dtype)
            return carry

        lax.fori_loop(0, rows // chunk, update, 0)
        if h == 0:
            each(n, lambda j: input_copy(other_dp(j), other_dp(j)).wait_recv())
        part[h] = jnp.dot(inputs[...], weights[:, span], preferred_element_type=jnp.float32).astype(part.dtype)
        each(n, lambda j: out_copy(h, other_dp(j), me).start())
        landed[h, me] = part[h, pl.ds(pl.multiple_of(me * nrows, nrows), nrows), :]
        stores.append(pltpu.make_async_copy(
            master.at[:, span], master_out.at[:, span], load_sem.at[6 + h]))
        stores[h].start()

    for h in range(2):
        each(n, lambda j: out_copy(h, other_dp(j), other_dp(j)).wait_recv())
        next_out[:, h * side:(h + 1) * side] = (
            jnp.sum(landed[h].astype(jnp.float32), axis=0) * (1.0 / math.sqrt(width))).astype(next_out.dtype)

    each(group, lambda j: pair_copy(peer(j), low).wait_send())
    each(group, lambda j: far_copy(peer(j), low).wait_send())
    each(group, lambda j: near_copy(peer(j), low).wait_send())
    for c in range(pieces):
        part_copy(c).wait_send()
    each(n, lambda j: input_copy(other_dp(j), me).wait_send())
    each(n, lambda j: sq_copy(other_dp(j), me).wait_send())
    each(sections, lambda j: sum_copy(other_section(j), sec).wait_send())
    for h in range(2):
        each(n, lambda j: out_copy(h, other_dp(j), me).wait_send())
        stores[h].wait()


def local(
    activations, tail_grads, tail_slots, master, moment1, moment2, overflow, clip_on, next_inputs
):
    n = lax.axis_size("dp")
    sections = lax.axis_size("section")
    tok = activations.shape[1]
    rows, cols = master.shape[1:]
    nrows = next_inputs.shape[1]
    group = n // 2
    step = min(rows, 256)
    pieces = rows // step
    f32, bf16 = jnp.float32, jnp.bfloat16
    vmem, anywhere, smem = (
        pl.BlockSpec(memory_space=m) for m in (pltpu.VMEM, pl.ANY, pltpu.SMEM))
    dma = pltpu.SemaphoreType.DMA
    new_master, next_out = pl.pallas_call(
        functools.partial(kernel, n, sections, step),
        out_shape=(
            jax.ShapeDtypeStruct((rows, cols), f32),
            jax.ShapeDtypeStruct((nrows, cols), bf16),
        ),
        in_specs=[anywhere, vmem, smem, anywhere, anywhere, anywhere, smem, smem, anywhere],
        out_specs=(anywhere, vmem),
        scratch_shapes=[
            pltpu.VMEM((group * tok, rows), bf16),
            pltpu.VMEM((group * tok, rows), bf16),
            pltpu.VMEM((group * tok, cols), bf16),
            pltpu.VMEM((rows, cols), f32),
            pltpu.VMEM((rows, cols), f32),
            pltpu.VMEM((rows, cols), f32),
            pltpu.VMEM((rows, cols), f32),
            pltpu.VMEM((pieces, step, cols), bf16),
            pltpu.VMEM((pieces, step, cols), bf16),
            pltpu.VMEM((rows, cols), bf16),
            pltpu.VMEM((n * nrows, rows), bf16),
            pltpu.VMEM((2, n * nrows, cols // 2), bf16),
            pltpu.VMEM((2, n, nrows, cols // 2), bf16),
            pltpu.VMEM((n, 8, 128), f32),
            pltpu.VMEM((sections, 8, 128), f32),
            pltpu.VMEM((8, 128), f32),
            pltpu.VMEM((8, 128), f32),
            dma((8,)),
            dma((group,)), dma((group,)),
            dma((group,)), dma((group,)),
            dma((group,)), dma((group,)),
            dma((pieces,)), dma((pieces,)),
            dma((n,)), dma((n,)),
            dma((2, n)), dma((2, n)),
            dma((n,)), dma((n,)),
            dma((sections,)), dma((sections,)),
        ],
        compiler_params=pltpu.CompilerParams(
            collective_id=0, has_side_effects=True, vmem_limit_bytes=56 * 1024 * 1024),
    )(
        activations[0], tail_grads[0], tail_slots[0], master[0], moment1[0], moment2[0],
        overflow, clip_on, next_inputs[0],
    )
    return (new_master[None], next_out[None])


def solution(mesh):
    return jax.shard_map(
        local,
        mesh=mesh,
        in_specs=(
            P("section", "dp", None),
            P("section", "dp", None),
            P("section", "dp", None),
            P("section", "dp", None),
            P("section", "dp", None),
            P("section", "dp", None),
            P("section", "dp"),
            P("section"),
            P("section", "dp", None),
        ),
        out_specs=(P("section", "dp", None), P("section", "dp", None)),
        check_vma=False,
    )
```

```python
import functools
import math

import jax
import jax.numpy as jnp
from jax import lax
from jax.experimental import pallas as pl
from jax.experimental.pallas import tpu as pltpu
from jax.sharding import PartitionSpec as P

MESH = pl.DeviceIdType.MESH
beta_one = 0.9
beta_two = 0.95
correct_one = 1.0 - 0.9**20
correct_two = 1.0 - 0.95**20
adam_eps = 1e-08
decay_rate = 0.1
learn_rate = 0.1


def remote(src, dst, send, recv, where):
    return pltpu.make_async_remote_copy(
        src_ref=src, dst_ref=dst, send_sem=send, recv_sem=recv, device_id=where,
        device_id_type=MESH,
    )


def kernel(
    n, sections, step,
    act, tails, slots, master_in, m1_in, m2_in, overflow, clip_on, nxt,
    master_out, next_out,
    far, near, paired, master, m1, m2, grad, psend, precv, weights, inputs, part, landed,
    sq_dp, sq_sec, sq_mine, sq_sum,
    load_sem, far_s, far_r, near_s, near_r, pair_s, pair_r, p_s, p_r, in_s, in_r, out_s, out_r,
    sd_s, sd_r, ss_s, ss_r,
):
    tok, width = act.shape
    rows, cols = master.shape
    nrows = nxt.shape[0]
    tail_count = slots.shape[-1]
    tail_tok = tok // tail_count
    group = n // 2
    me = lax.axis_index("dp")
    sec = lax.axis_index("section")
    half = me // group
    low = lax.rem(me, group)
    other = 1 - half
    pieces = rows // step

    def each(count, body):
        lax.fori_loop(1, count, lambda j, c: (body(j), c)[1], 0)

    barrier = pltpu.get_barrier_semaphore()
    each(n, lambda j: pl.semaphore_signal(
        barrier, inc=1, device_id={"dp": lax.rem(me + j, n)}, device_id_type=MESH))
    each(sections, lambda j: pl.semaphore_signal(
        barrier, inc=1, device_id={"section": lax.rem(sec + j, sections)}, device_id_type=MESH))

    def feature(dev):
        return pl.ds(pl.multiple_of(dev * rows, rows), rows)

    def block(ref, index, size):
        return ref.at[pl.ds(pl.multiple_of(index * size, size), size)]

    loads = [
        pltpu.make_async_copy(
            act.at[:, feature(other * group + low)], block(far, low, tok), load_sem.at[0]),
        pltpu.make_async_copy(
            act.at[:, feature(me)], block(near, low, tok), load_sem.at[1]),
        pltpu.make_async_copy(
            nxt.at[:, feature(me)], block(inputs, me, nrows), load_sem.at[2]),
        pltpu.make_async_copy(master_in, master, load_sem.at[3]),
        pltpu.make_async_copy(m1_in, m1, load_sem.at[4]),
        pltpu.make_async_copy(m2_in, m2, load_sem.at[5]),
    ]
    for load in loads:
        load.start()

    mine = pl.multiple_of(low * tok, tok)
    for k in range(tail_count):
        value = tails[0:tail_tok, :]
        for t in range(1, tail_count):
            value = jnp.where(
                slots[0, t] == k, tails[t * tail_tok:(t + 1) * tail_tok, :], value)
        paired[pl.ds(mine + k * tail_tok, tail_tok), :] = value

    pl.semaphore_wait(barrier, n - 1 + sections - 1)

    def peer(j):
        return lax.rem(low + j, group)

    def pair_copy(to, slot):
        return remote(block(paired, low, tok), block(paired, slot, tok), pair_s.at[to],
                      pair_r.at[slot], {"dp": half * group + to})

    def far_copy(to, slot):
        return remote(act.at[:, feature(other * group + to)], block(far, slot, tok),
                      far_s.at[to], far_r.at[slot], {"dp": half * group + to})

    def near_copy(to, slot):
        return remote(act.at[:, feature(half * group + to)], block(near, slot, tok),
                      near_s.at[to], near_r.at[slot], {"dp": half * group + to})

    inner = low + 1 - 2 * lax.rem(low, 2)
    outer = group // 2

    def across(j):
        return lax.rem(low + 2 * j, group)


    def diagonal(j):
        return lax.rem(inner + 2 * j, group)

    each(outer, lambda j: far_copy(across(j), low).start())
    each(outer, lambda j: far_copy(diagonal(j), low).start())
    far_copy(inner, low).start()
    each(group, lambda j: pair_copy(peer(j), low).start())
    each(outer, lambda j: near_copy(across(j), low).start())
    each(outer, lambda j: near_copy(diagonal(j), low).start())
    near_copy(inner, low).start()

    contract = (((0,), (0,)), ((), ()))

    loads[0].wait()
    each(group, lambda j: pair_copy(peer(j), peer(j)).wait_recv())
    each(group, lambda j: far_copy(peer(j), peer(j)).wait_recv())

    def part_copy(c):
        return remote(psend.at[c], precv.at[c], p_s.at[c], p_r.at[c],
                      {"dp": other * group + low})

    for c in range(pieces):
        psend[c] = lax.dot_general(
            far[:, c * step:(c + 1) * step], paired[...], contract,
            preferred_element_type=jnp.float32).astype(psend.dtype)
        part_copy(c).start()

    def input_copy(to, slot):
        return remote(nxt.at[:, feature(to)], block(inputs, slot, nrows), in_s.at[to],
                      in_r.at[slot], {"dp": to})

    def other_dp(j):
        return lax.rem(me + j, n)

    loads[1].wait()
    each(group, lambda j: near_copy(peer(j), peer(j)).wait_recv())
    for c in range(pieces):
        grad[c * step:(c + 1) * step, :] = lax.dot_general(
            near[:, c * step:(c + 1) * step], paired[...], contract,
            preferred_element_type=jnp.float32)

    scale = 1.0 / (tok * n)
    chunk = 32
    squares = jnp.zeros((8, cols), jnp.float32)
    for c in range(pieces):
        part_copy(c).wait_recv()

        def add(i, total):
            at = pl.multiple_of(i * chunk, chunk)
            g = (grad[pl.ds(c * step + at, chunk), :]
                 + precv[c, pl.ds(at, chunk), :].astype(jnp.float32)) * scale
            grad[pl.ds(c * step + at, chunk), :] = g
            return total + jnp.sum((g * g).reshape(chunk // 8, 8, cols), axis=0)

        squares = lax.fori_loop(0, step // chunk, add, squares)

    tile = squares[:, 0:128]
    for c in range(1, cols // 128):
        tile = tile + squares[:, c * 128:(c + 1) * 128]
    keep = jnp.where(overflow[0, 0] == 0, 1.0, 0.0)
    tile = tile * keep
    sq_mine[...] = tile

    def sq_copy(to, slot):
        return remote(sq_mine, sq_dp.at[slot], sd_s.at[to], sd_r.at[slot], {"dp": to})

    def sum_copy(to, slot):
        return remote(sq_sum, sq_sec.at[slot], ss_s.at[to], ss_r.at[slot], {"section": to})

    def other_section(j):
        return lax.rem(sec + j, sections)

    each(n, lambda j: sq_copy(other_dp(j), me).start())
    each(n, lambda j: input_copy(other_dp(j), me).start())
    sq_dp[me] = tile
    for load in loads[2:]:
        load.wait()
    each(n, lambda j: sq_copy(other_dp(j), other_dp(j)).wait_recv())
    tile = jnp.sum(sq_dp[...], axis=0)
    sq_sum[...] = tile
    each(sections, lambda j: sum_copy(other_section(j), sec).start())
    sq_sec[sec] = tile
    each(sections, lambda j: sum_copy(other_section(j), other_section(j)).wait_recv())
    sumsq = jnp.sum(jnp.sum(sq_sec[...], axis=0), keepdims=True)
    factor = jnp.where(clip_on[0] == 1, 1.0 / jnp.maximum(jnp.sqrt(sumsq), 1.0), 1.0)
    side = cols // 2
    factor = jnp.broadcast_to(factor, (1, side))
    rate = learn_rate * keep

    def out_copy(h, to, slot):
        return remote(part.at[h, pl.ds(pl.multiple_of(to * nrows, nrows), nrows)],
                      landed.at[h, slot], out_s.at[h, to], out_r.at[h, slot], {"dp": to})

    stores = []
    for h in range(2):
        span = slice(h * side, (h + 1) * side)

        def update(i, carry):
            at = pl.ds(pl.multiple_of(i * chunk, chunk), chunk)
            clipped = grad[at, span] * factor
            old = master[at, span]
            m_next = beta_one * m1[at, span] + (1.0 - beta_one) * clipped
            v_next = beta_two * m2[at, span] + (1.0 - beta_two) * (clipped * clipped)
            change = (m_next * (1.0 / correct_one)) / (
                jnp.sqrt(v_next * (1.0 / correct_two)) + adam_eps) + decay_rate * old
            new = old - rate * change
            master[at, span] = new
            weights[at, span] = new.astype(weights.dtype)
            return carry

        lax.fori_loop(0, rows // chunk, update, 0)
        if h == 0:
            each(n, lambda j: input_copy(other_dp(j), other_dp(j)).wait_recv())
        part[h] = jnp.dot(inputs[...], weights[:, span], preferred_element_type=jnp.float32).astype(part.dtype)
        each(n, lambda j: out_copy(h, other_dp(j), me).start())
        landed[h, me] = part[h, pl.ds(pl.multiple_of(me * nrows, nrows), nrows), :]
        stores.append(pltpu.make_async_copy(
            master.at[:, span], master_out.at[:, span], load_sem.at[6 + h]))
        stores[h].start()

    for h in range(2):
        each(n, lambda j: out_copy(h, other_dp(j), other_dp(j)).wait_recv())
        next_out[:, h * side:(h + 1) * side] = (
            jnp.sum(landed[h].astype(jnp.float32), axis=0) * (1.0 / math.sqrt(width))).astype(next_out.dtype)

    each(group, lambda j: pair_copy(peer(j), low).wait_send())
    each(group, lambda j: far_copy(peer(j), low).wait_send())
    each(group, lambda j: near_copy(peer(j), low).wait_send())
    for c in range(pieces):
        part_copy(c).wait_send()
    each(n, lambda j: input_copy(other_dp(j), me).wait_send())
    each(n, lambda j: sq_copy(other_dp(j), me).wait_send())
    each(sections, lambda j: sum_copy(other_section(j), sec).wait_send())
    for h in range(2):
        each(n, lambda j: out_copy(h, other_dp(j), me).wait_send())
        stores[h].wait()


def local(
    activations, tail_grads, tail_slots, master, moment1, moment2, overflow, clip_on, next_inputs
):
    n = lax.axis_size("dp")
    sections = lax.axis_size("section")
    tok = activations.shape[1]
    rows, cols = master.shape[1:]
    nrows = next_inputs.shape[1]
    group = n // 2
    step = min(rows, 256)
    pieces = rows // step
    f32, bf16 = jnp.float32, jnp.bfloat16
    vmem, anywhere, smem = (
        pl.BlockSpec(memory_space=m) for m in (pltpu.VMEM, pl.ANY, pltpu.SMEM))
    dma = pltpu.SemaphoreType.DMA
    new_master, next_out = pl.pallas_call(
        functools.partial(kernel, n, sections, step),
        out_shape=(
            jax.ShapeDtypeStruct((rows, cols), f32),
            jax.ShapeDtypeStruct((nrows, cols), bf16),
        ),
        in_specs=[anywhere, vmem, smem, anywhere, anywhere, anywhere, smem, smem, anywhere],
        out_specs=(anywhere, vmem),
        scratch_shapes=[
            pltpu.VMEM((group * tok, rows), bf16),
            pltpu.VMEM((group * tok, rows), bf16),
            pltpu.VMEM((group * tok, cols), bf16),
            pltpu.VMEM((rows, cols), f32),
            pltpu.VMEM((rows, cols), f32),
            pltpu.VMEM((rows, cols), f32),
            pltpu.VMEM((rows, cols), f32),
            pltpu.VMEM((pieces, step, cols), bf16),
            pltpu.VMEM((pieces, step, cols), bf16),
            pltpu.VMEM((rows, cols), bf16),
            pltpu.VMEM((n * nrows, rows), bf16),
            pltpu.VMEM((2, n * nrows, cols // 2), bf16),
            pltpu.VMEM((2, n, nrows, cols // 2), bf16),
            pltpu.VMEM((n, 8, 128), f32),
            pltpu.VMEM((sections, 8, 128), f32),
            pltpu.VMEM((8, 128), f32),
            pltpu.VMEM((8, 128), f32),
            dma((8,)),
            dma((group,)), dma((group,)),
            dma((group,)), dma((group,)),
            dma((group,)), dma((group,)),
            dma((pieces,)), dma((pieces,)),
            dma((n,)), dma((n,)),
            dma((2, n)), dma((2, n)),
            dma((n,)), dma((n,)),
            dma((sections,)), dma((sections,)),
        ],
        compiler_params=pltpu.CompilerParams(
            collective_id=0, has_side_effects=True, vmem_limit_bytes=56 * 1024 * 1024),
    )(
        activations[0], tail_grads[0], tail_slots[0], master[0], moment1[0], moment2[0],
        overflow, clip_on, next_inputs[0],
    )
    return (new_master[None], next_out[None])


def solution(mesh):
    return jax.shard_map(
        local,
        mesh=mesh,
        in_specs=(
            P("section", "dp", None),
            P("section", "dp", None),
            P("section", "dp", None),
            P("section", "dp", None),
            P("section", "dp", None),
            P("section", "dp", None),
            P("section", "dp"),
            P("section"),
            P("section", "dp", None),
        ),
        out_specs=(P("section", "dp", None), P("section", "dp", None)),
        check_vma=False,
    )
```
